128 devices in a mesh: region: 8 (over y, core), member: 16 (over x, z).
Axes of the slice: x: 4, y: 4, z: 4, core: 2. Of those that a mesh axis runs over, the one named last changes fastest.
Arguments:
- interface_load: float32 [2048, 1024], P(('region', 'member')), may hold values from -23 to 23
- schur_values: float32 [2048, 16, 4096], P(('region', 'member')), may hold values from -0.04 to 2.04, as said below
- schur_columns: int32 [2048, 16], P(('region', 'member')), may hold values from 0 to 2047, as said below
- coupling: float32 [256, 1024, 512], P(('region', 'member')), may hold values from -0.25 to 0.25
- layer_inverse: float32 [256, 1024, 1024], P(('region', 'member')), may hold values from -0.1875 to 0.1875
- interior_load: float32 [256, 16, 1024], P(('region', 'member')), may hold values from -6 to 6
- adjacency: int32 [256, 8], P(('region', 'member')), may hold values from 0 to 2047, as said below
- live_counts: int32 [256], P(('region', 'member')), may hold values from 4 to 8, as said below
Outputs:
- solution: float32 [2048, 1024], P(('region', 'member'))
- residual: float32 [2048, 1024], P(('region', 'member'))
- interior: float32 [256, 16, 1024], P(('region', 'member'))
The draws below stay inside these ranges and needn't reach their ends.
Inputs may be any that keep to these rules, and one draw needn't show every extreme that they name: `schur_columns`: block row i of region g = i // 256 stores its own block in slot 0; slot 1 holds a block of region g - 1 and slot 2 one of region g + 1 (of region g itself at the ends), each such block named by exactly one row of region g; the other slots name blocks of regions g - 1 to g + 1 that exist. Call the blocks b with (b % 256) // 16 = m the blocks of member index m; the rows of one device name at most 32 distinct blocks of any one member index, and exactly 32 for some member index on every device of a region other than the first and last. `schur_values`: the slot 0 block of each row is 2 times the identity plus small entries; all other entries are small. `adjacency`: the substructures of device d (those with index // 2 equal to d) name blocks of regions r - 1 to r + 1 that exist, where r = d // 16; slots past the live count hold such blocks too. `live_counts`: every substructure with an even index has all 8 slots live.
All inputs are finite; a program needn't handle non-finite values.
Results may differ from the reference program's by a relative error of at most 0.0003.
Values sent between devices are 32-bit elements; how exact they have to be, the bound alone decides.
No kernel may reach another device: no remote copies, remote signals or barrier semaphores. Data moves between devices by JAX's collectives and lax.ppermute only.
A program may use at most 128 MiB of HBM per device.

```python
import jax
import jax.numpy as jnp
from jax import lax

NB = 64
CASES = 16
ITERS = 2
K_SLOTS = 16
A_PAD = 8
IB_DEV = 16
SUB_DEV = 2
NI = 1024
IB_REG = 256
IB_ALL = 2048
SUBS = 256
N_REGION = 8
N_MEMBER = 16


def draw_interface_load(key, part):
    key = jax.random.fold_in(key, 5)
    row_ids = jnp.arange(IB_ALL, dtype=jnp.float32)[:, None]
    ramp = 0.6 + 1.2 * row_ids / max(IB_ALL - 1, 1)
    rough = jnp.exp(jax.random.uniform(jax.random.fold_in(key, 1), (IB_ALL, 1), jnp.float32, -1.15, 1.15))
    values = jnp.clip(jax.random.normal(key, (IB_ALL, CASES * NB), jnp.float32), -4.0, 4.0)
    return (values * ramp * rough).astype(jnp.float32)


def draw_schur_values(key, part):
    key = jax.random.fold_in(key, 7)
    small = jax.random.uniform(key, (IB_ALL, K_SLOTS, NB * NB), jnp.float32, -0.04, 0.04)
    flat = jnp.arange(NB * NB, dtype=jnp.int32)
    diagonal = (flat // NB == flat % NB).astype(jnp.float32)
    slot_zero = (jnp.arange(K_SLOTS, dtype=jnp.int32) == 0).astype(jnp.float32)
    return (small + 2.0 * slot_zero[None, :, None] * diagonal[None, None, :]).astype(jnp.float32)


def draw_schur_columns(key, part):
    key = jax.random.fold_in(key, 11)
    half = (IB_DEV + 1) // 2
    row_ids = jnp.arange(IB_ALL, dtype=jnp.int32)[:, None]
    region_ids = row_ids // IB_REG
    within = row_ids % IB_REG
    own_member = within // IB_DEV
    offset = within % IB_DEV
    first_shift = jax.random.randint(jax.random.fold_in(key, 1), (N_REGION,), 1, N_MEMBER, dtype=jnp.int32)
    extra = jax.random.randint(jax.random.fold_in(key, 2), (N_REGION,), 1, N_MEMBER - 1, dtype=jnp.int32)
    second_shift = 1 + (first_shift - 1 + extra) % (N_MEMBER - 1)
    member_one = (own_member + first_shift[region_ids[:, 0]][:, None]) % N_MEMBER
    member_two = (own_member + second_shift[region_ids[:, 0]][:, None]) % N_MEMBER
    below_region = jnp.where(region_ids > 0, region_ids - 1, region_ids)
    above_region = jnp.where(region_ids < N_REGION - 1, region_ids + 1, region_ids)
    below = below_region * IB_REG + member_one * IB_DEV + offset
    above = above_region * IB_REG + member_two * IB_DEV + offset
    third = region_ids * IB_REG + member_one * IB_DEV + offset % half
    fourth = above_region * IB_REG + member_one * IB_DEV + offset % half
    lowest = jnp.maximum(region_ids - 1, 0)
    count_regions = jnp.minimum(region_ids + 2, N_REGION) - lowest
    bits_region = jax.random.randint(jax.random.fold_in(key, 3), (IB_ALL, K_SLOTS), 0, 1 << 20, dtype=jnp.int32)
    bits_member = jax.random.randint(jax.random.fold_in(key, 4), (IB_ALL, K_SLOTS), 0, N_MEMBER, dtype=jnp.int32)
    bits_offset = jax.random.randint(jax.random.fold_in(key, 5), (IB_ALL, K_SLOTS), 0, half, dtype=jnp.int32)
    anywhere = (lowest + bits_region % count_regions) * IB_REG + bits_member * IB_DEV + bits_offset
    slot_ids = jnp.arange(K_SLOTS, dtype=jnp.int32)[None, :]
    picked = jnp.where(slot_ids == 0, row_ids, jnp.where(slot_ids == 1, below, jnp.where(slot_ids == 2, above, jnp.where(slot_ids == 3, third, jnp.where(slot_ids == 4, fourth, anywhere)))))
    return picked.astype(jnp.int32)


def draw_adjacency(key, part):
    key = jax.random.fold_in(key, 13)
    sub_ids = jnp.arange(SUBS, dtype=jnp.int32)[:, None]
    region_ids = sub_ids // SUB_DEV // N_MEMBER
    lowest = jnp.maximum(region_ids - 1, 0) * IB_REG
    highest = jnp.minimum(region_ids + 2, N_REGION) * IB_REG
    random_bits = jax.random.randint(key, (SUBS, A_PAD), 0, 1 << 20, dtype=jnp.int32)
    return (lowest + random_bits % (highest - lowest)).astype(jnp.int32)


def draw_live_counts(key, part):
    key = jax.random.fold_in(key, 17)
    counts = jax.random.randint(key, (SUBS,), (A_PAD + 1) // 2, A_PAD + 1, dtype=jnp.int32)
    sub_ids = jnp.arange(SUBS, dtype=jnp.int32)
    return jnp.where(sub_ids % 2 == 0, A_PAD, counts).astype(jnp.int32)


def block_scale(stream_key, shape, cuts, smallest, high):
    def one(position, shards_of):
        draws = jax.random.uniform(jax.random.fold_in(jax.random.fold_in(stream_key, 6), position), (shards_of,), jnp.float32, smallest / len(cuts), high / len(cuts))
        return jnp.repeat(jnp.exp(draws), shape[position] // shards_of).reshape((-1,) + (1,) * (len(shape) - position - 1))

    level = one(*cuts[0])
    for cut in cuts[1:]:
        level = level * one(*cut)
    return level


def noise(key, extent, scale, limit, pieces=(), kind=jnp.bfloat16):
    values = scale * jax.random.normal(key, extent, jnp.float32)
    if pieces:
        values = values * block_scale(key, extent, pieces, -0.22, 0.18)
    return jnp.clip(values, -limit, limit).astype(kind)


def setup_inputs(seed: int = 0) -> dict:
    streams_of = jax.random.split(jax.random.key(seed), 9)
    return {
        "interface_load": draw_interface_load(jax.random.fold_in(streams_of[8], 71), 0),
        "schur_values": draw_schur_values(jax.random.fold_in(streams_of[8], 71), 0),
        "schur_columns": draw_schur_columns(jax.random.fold_in(streams_of[8], 71), 0),
        "coupling": noise(streams_of[3], (SUBS, NI, A_PAD * NB), (A_PAD * NB) ** -0.5, 0.25, ((0, 128),), jnp.float32),
        "layer_inverse": noise(streams_of[4], (SUBS, NI, NI), NI ** -0.5, 0.1875, ((0, 128),), jnp.float32),
        "interior_load": noise(streams_of[5], (SUBS, CASES, NI), 1.0, 6.0, ((0, 128),), jnp.float32),
        "adjacency": draw_adjacency(jax.random.fold_in(streams_of[8], 71), 0),
        "live_counts": draw_live_counts(jax.random.fold_in(streams_of[8], 71), 0),
    }


HIGHEST_MODE = lax.Precision.HIGHEST


def apply_schur(values, column_ids, field):
    blocks = field.reshape(field.shape[0], CASES, NB)[column_ids]
    matrices = values.reshape(values.shape[0], values.shape[1], NB, NB)
    result = jnp.einsum("ikrq,ikcq->icr", matrices, blocks, precision=HIGHEST_MODE)
    return result.reshape(result.shape[0], CASES * NB)


def case_partial(left, right):
    return jnp.sum((left * right).reshape(-1, CASES, NB), axis=(0, 2))


def widen(factor):
    return jnp.repeat(factor, NB)[None, :]


def recover(field, slot_ids, live_counts, coupling, layer_inverse, interior_load):
    picked = field.reshape(field.shape[0], CASES, NB)[slot_ids]
    positions = jnp.arange(picked.shape[1], dtype=jnp.int32)
    live_mask = (positions[None, :] < live_counts[:, None]).astype(jnp.float32)
    picked = picked * live_mask[:, :, None, None]
    matrices = coupling.reshape(coupling.shape[0], coupling.shape[1], -1, NB)
    reduced = interior_load - jnp.einsum("snaq,sacq->scn", matrices, picked, precision=HIGHEST_MODE)
    return jnp.einsum("snm,scm->scn", layer_inverse, reduced, precision=HIGHEST_MODE)


def reference(interface_load, schur_values, schur_columns, coupling, layer_inverse, interior_load, adjacency, live_counts):
    solution = jnp.zeros_like(interface_load)
    residual = interface_load
    direction = interface_load
    norm_now = case_partial(residual, residual)
    for iteration in range(ITERS):
        image = apply_schur(schur_values, schur_columns, direction)
        step_size = norm_now / case_partial(direction, image)
        solution = solution + widen(step_size) * direction
        residual = residual - widen(step_size) * image
        if iteration + 1 < ITERS:
            norm_next = case_partial(residual, residual)
            direction = residual + widen(norm_next / norm_now) * direction
            norm_now = norm_next
    interior = recover(solution, adjacency, live_counts, coupling, layer_inverse, interior_load)
    return (solution, residual, interior)
```

```python
import jax
import jax.numpy as jnp
from jax import lax
from jax.experimental import pallas as pl
from jax.experimental.pallas import tpu as pltpu
from jax.sharding import PartitionSpec as P

NB = 64
CASES = 16
LANES = 128
AXES = ("y", "core", "x", "z")
SIZES = (4, 2, 4, 4)
ORDER = (0, 1, 3, 2)
WINDOW = 768
NT = (((1,), (1,)), ((), ()))

PLACES = [
    (y, c, x, z)
    for y in range(SIZES[0])
    for c in range(SIZES[1])
    for x in range(SIZES[2])
    for z in range(SIZES[3])
]


def flat(y, c, x, z):
    return ((y * SIZES[1] + c) * SIZES[2] + x) * SIZES[3] + z


def permute(value, target):
    pairs = []
    for place in PLACES:
        goal = target(*place)
        if goal is not None:
            pairs.append((flat(*place), flat(*goal)))
    return lax.ppermute(value, AXES, pairs)


def far(y, c, x, z):
    if c == 1:
        return (y + 1, 0, x, z) if y + 1 < SIZES[0] else None
    return (y - 1, 1, x, z) if y > 0 else None


def partner(y, c, x, z):
    return (y, 1 - c, x, z)


def along_first(step):
    return lambda y, c, x, z: (y, c, x, (z - step) % 4) if c == 0 else (y, c, (x - step) % 4, z)


def along_second(step):
    return lambda y, c, x, z: (y, c, (x - step) % 4, z) if c == 0 else (y, c, x, (z - step) % 4)


def exchange(own):
    line = [own] + [permute(own, along_first(k)) for k in ORDER[1:]]
    line = jnp.concatenate(line)
    plane = [line] + [permute(line, along_second(k)) for k in ORDER[1:]]
    others = [permute(piece, far) for piece in plane]
    pair = [permute(piece, partner) for piece in plane]
    return jnp.concatenate(plane + others + pair)


def locate(ids, region, x, z):
    goal = ids // 256
    member = ids % 256 // 16
    dx = (member // 4 - x) % 4
    dz = (member % 4 - z) % 4
    px = dx ^ (dx >> 1)
    pz = dz ^ (dz >> 1)
    odd = goal % 2 == 1
    first = jnp.where(odd, pz, px)
    second = jnp.where(odd, px, pz)
    group = jnp.where(goal == region, 0, jnp.where(goal == (region ^ 1), 2, 1))
    return ((group * 4 + first) * 4 + second) * 16 + ids % 16


def split(value):
    high = value.astype(jnp.bfloat16)
    low = (value - high.astype(jnp.float32)).astype(jnp.bfloat16)
    return high, low


def lane_ids(rows):
    return lax.broadcasted_iota(jnp.int32, (rows, LANES), 1)


def merge_halves(left, right):
    low_half = lane_ids(left.shape[0]) < NB
    first = jnp.where(low_half, left, pltpu.roll(right, NB, 1))
    second = jnp.where(low_half, pltpu.roll(left, NB, 1), right)
    return first, second


def prepare_kernel(values_ref, out_ref, rows_ref):
    lanes = lane_ids(8)
    subs = lax.broadcasted_iota(jnp.int32, (8, LANES), 0)
    for pair in range(32):
        cut = slice(pair * LANES, (pair + 1) * LANES)
        upper = values_ref[0, 0:8, cut]
        lower = values_ref[0, 8:16, cut]
        own = (subs == 0) & ((lanes == 2 * pair) | (lanes == NB + 2 * pair + 1))
        upper = jnp.where(own, upper - 2.0, upper)
        first, second = merge_halves(upper, lower)
        rows_ref[pl.ds(2 * pair, 8, stride=NB), :] = first
        rows_ref[pl.ds(2 * pair + 1, 8, stride=NB), :] = second
    for k in range(8):
        high, low = split(rows_ref[k * NB : (k + 1) * NB, :])
        out_ref[0, 0:NB, k * LANES : (k + 1) * LANES] = high
        out_ref[0, NB : 2 * NB, k * LANES : (k + 1) * LANES] = low


def prepare(values):
    rows = values.shape[0]
    return pl.pallas_call(
        prepare_kernel,
        grid=(rows,),
        in_specs=[pl.BlockSpec((1, 16, 4096), lambda i: (i, 0, 0))],
        out_specs=pl.BlockSpec((1, 128, 1024), lambda i: (i, 0, 0)),
        out_shape=jax.ShapeDtypeStruct((rows, 128, 1024), jnp.bfloat16),
        scratch_shapes=[pltpu.VMEM((512, LANES), jnp.float32)],
        compiler_params=pltpu.CompilerParams(vmem_limit_bytes=8 * 2**20),
        cost_estimate=pl.CostEstimate(flops=2**24, bytes_accessed=2**23, transcendentals=0),
        name="prepare",
    )(values)


def apply_rows(places_ref, window_ref, matrices_ref, x_ref, out_ref):
    low_half = lane_ids(8) < NB
    for row in range(16):
        for k in range(8):
            left = window_ref[places_ref[row * 16 + k]]
            right = window_ref[places_ref[row * 16 + k + 8]]
            high, low = split(jnp.concatenate(merge_halves(left, right)))
            x_ref[row % 2, 0:16, k * LANES : (k + 1) * LANES] = high
            x_ref[row % 2, 16:32, k * LANES : (k + 1) * LANES] = low
        product = lax.dot_general(
            x_ref[row % 2], matrices_ref[row], NT, preferred_element_type=jnp.float32
        )
        both = product[0:16] + product[16:32]
        both = both + pltpu.roll(both, NB, 1)
        out_ref[row] = jnp.where(low_half, both[0:8], both[8:16])


def first_kernel(places_ref, window_ref, matrices_ref, image_ref, x_ref):
    apply_rows(places_ref, window_ref, matrices_ref, x_ref, image_ref)


def second_kernel(
    places_ref, window_ref, matrices_ref, load_ref, image_ref, twice_ref, sums_ref, x_ref
):
    apply_rows(places_ref, window_ref, matrices_ref, x_ref, twice_ref)
    load, image, twice = load_ref[...], image_ref[...], twice_ref[...]
    lanes = lane_ids(8)
    low_half = lanes < NB
    packed = jnp.zeros((8, LANES), jnp.float32)
    products = (load * load, load * image, image * image, load * twice, image * twice)
    for place, product in enumerate(products):
        tile = jnp.sum(product, axis=0)
        left = jnp.sum(jnp.where(low_half, tile, 0.0), axis=1, keepdims=True)
        right = jnp.sum(jnp.where(low_half, 0.0, tile), axis=1, keepdims=True)
        packed = jnp.where(lanes == place, left, packed)
        packed = jnp.where(lanes == NB + place, right, packed)
    sums_ref[...] = packed


VMEM_SPEC = pl.BlockSpec(memory_space=pltpu.VMEM)
SMEM_SPEC = pl.BlockSpec(memory_space=pltpu.SMEM)
APPLY_COST = pl.CostEstimate(flops=2**27, bytes_accessed=2**23, transcendentals=0)


def apply_first(places, window, matrices):
    return pl.pallas_call(
        first_kernel,
        in_specs=[SMEM_SPEC, VMEM_SPEC, VMEM_SPEC],
        out_specs=VMEM_SPEC,
        out_shape=jax.ShapeDtypeStruct((16, 8, LANES), jnp.float32),
        scratch_shapes=[pltpu.VMEM((2, 32, 1024), jnp.bfloat16)],
        compiler_params=pltpu.CompilerParams(vmem_limit_bytes=16 * 2**20),
        cost_estimate=APPLY_COST,
        name="apply_first",
    )(places, window, matrices)


def apply_second(places, window, matrices, load, image):
    return pl.pallas_call(
        second_kernel,
        in_specs=[SMEM_SPEC] + [VMEM_SPEC] * 4,
        out_specs=[VMEM_SPEC] * 2,
        out_shape=[
            jax.ShapeDtypeStruct((16, 8, LANES), jnp.float32),
            jax.ShapeDtypeStruct((8, LANES), jnp.float32),
        ],
        scratch_shapes=[pltpu.VMEM((2, 32, 1024), jnp.bfloat16)],
        compiler_params=pltpu.CompilerParams(vmem_limit_bytes=16 * 2**20),
        cost_estimate=APPLY_COST,
        name="apply_second",
    )(places, window, matrices, load, image)


def couple_kernel(slots_ref, live_ref, first_ref, second_ref, coupling_ref, load_ref, out_ref, x_ref, rows_ref):
    sub = pl.program_id(0)

    @pl.when(pl.program_id(1) == 0)
    def _():
        for t in range(4):
            for which, ref in enumerate((first_ref, second_ref)):
                tiles = []
                for slot in (2 * t, 2 * t + 1):
                    tile = ref[slots_ref[sub * 8 + slot]]
                    tiles.append(jnp.where(slot < live_ref[sub], tile, 0.0))
                even, odd = merge_halves(*tiles)
                rows_ref[t, which, pl.ds(0, 8, stride=2), :] = even
                rows_ref[t, which, pl.ds(1, 8, stride=2), :] = odd
                high, low = split(rows_ref[t, which])
                x_ref[16 * which : 16 * which + 16, t * LANES : (t + 1) * LANES] = high
                x_ref[32 + 16 * which : 48 + 16 * which, t * LANES : (t + 1) * LANES] = low

    high, low = split(coupling_ref[0])
    main = lax.dot_general(x_ref[...], high, NT, preferred_element_type=jnp.float32)
    rest = lax.dot_general(x_ref[0:32], low, NT, preferred_element_type=jnp.float32)
    out_ref[0, 16:48, :] = main[0:32] + main[32:64] + rest
    out_ref[0, 0:16, :] = load_ref[0]


def couple(slots, live, first, second, coupling, load):
    cut = 512
    return pl.pallas_call(
        couple_kernel,
        grid=(2, 1024 // cut),
        in_specs=[
            SMEM_SPEC,
            SMEM_SPEC,
            VMEM_SPEC,
            VMEM_SPEC,
            pl.BlockSpec((1, cut, 512), lambda s, n: (s, n, 0)),
            pl.BlockSpec((1, 16, cut), lambda s, n: (s, 0, n)),
        ],
        out_specs=pl.BlockSpec((1, 48, cut), lambda s, n: (s, 0, n)),
        out_shape=jax.ShapeDtypeStruct((2, 48, 1024), jnp.float32),
        scratch_shapes=[pltpu.VMEM((64, 512), jnp.bfloat16), pltpu.VMEM((4, 2, 16, LANES), jnp.float32)],
        compiler_params=pltpu.CompilerParams(vmem_limit_bytes=16 * 2**20),
        cost_estimate=pl.CostEstimate(flops=2**28, bytes_accessed=2**22, transcendentals=0),
        name="couple",
    )(slots, live, first, second, coupling, load)


def layers_kernel(reduced_ref, inverse_ref, out_ref):
    top, bottom = split(reduced_ref[0])
    high, low = split(inverse_ref[0])
    main = lax.dot_general(
        jnp.concatenate([top, bottom]), high, NT, preferred_element_type=jnp.float32
    )
    rest = lax.dot_general(top, low, NT, preferred_element_type=jnp.float32)
    out_ref[0] = main[0:48] + main[48:96] + rest


def layers(reduced, inverse):
    cut = 256
    return pl.pallas_call(
        layers_kernel,
        grid=(2, 1024 // cut),
        in_specs=[
            pl.BlockSpec((1, 48, 1024), lambda s, n: (s, 0, 0)),
            pl.BlockSpec((1, cut, 1024), lambda s, n: (s, n, 0)),
        ],
        out_specs=pl.BlockSpec((1, 48, cut), lambda s, n: (s, 0, n)),
        out_shape=jax.ShapeDtypeStruct((2, 48, 1024), jnp.float32),
        compiler_params=pltpu.CompilerParams(vmem_limit_bytes=16 * 2**20),
        cost_estimate=pl.CostEstimate(flops=2**29, bytes_accessed=2**23, transcendentals=0),
        name="layers",
    )(reduced, inverse)


def finish_kernel(
    sums_ref, load_ref, image_ref, twice_ref, parts_ref, solution_ref, residual_ref, interior_ref, tiles_ref, cases_ref
):
    lanes = lane_ids(8)
    low_half = lanes < NB
    packed = jnp.sum(sums_ref[...], axis=0)

    def pick(place):
        left = jnp.sum(jnp.where(lanes == place, packed, 0.0), axis=1, keepdims=True)
        right = jnp.sum(jnp.where(lanes == NB + place, packed, 0.0), axis=1, keepdims=True)
        return jnp.where(low_half, left, right)

    uu, ue, ee, uf, ef = [pick(place) for place in range(5)]
    inner = 2.0 * uu + ue
    step = uu / inner
    along = ue / inner
    beta = step * (ee / inner) - along * along
    norm = beta * uu
    mix = along + beta
    length = mix * mix * uu - 2.0 * mix * step * ue + step * step * ee
    cross = mix * mix * ue - mix * step * (uf + ee) + step * step * ef
    last = norm / (2.0 * length + cross)
    on_load = step + last * mix
    on_image = -last * step
    rest_load = along - 2.0 * last * mix
    rest_image = -step - last * (mix - 2.0 * step)
    rest_twice = last * step

    rows = load_ref.shape[0]
    load, image, twice = load_ref[...], image_ref[...], twice_ref[...]
    for out_ref, value in (
        (solution_ref, on_load[None] * load + on_image[None] * image),
        (
            residual_ref,
            rest_load[None] * load + rest_image[None] * image + rest_twice[None] * twice,
        ),
    ):
        tiles_ref[...] = value.reshape(rows * 8, LANES)
        for s in range(8):
            out_ref[:, s * LANES : (s + 1) * LANES] = tiles_ref[pl.ds(s, rows, stride=8), :]
    for place, factor in enumerate((on_load, on_image)):
        for h in range(2):
            spread = jnp.broadcast_to(factor[:, h * NB : h * NB + 1], (8, LANES))
            cases_ref[place, pl.ds(h, 8, stride=2), :] = spread
    own, other = cases_ref[0][:, 0:1], cases_ref[1][:, 0:1]
    for sub in range(2):
        interior_ref[sub] = (
            parts_ref[sub, 0:16] - own * parts_ref[sub, 16:32] - other * parts_ref[sub, 32:48]
        )


def finish(sums, load, image, twice, parts):
    return pl.pallas_call(
        finish_kernel,
        in_specs=[VMEM_SPEC] * 5,
        out_specs=[VMEM_SPEC] * 3,
        out_shape=[
            jax.ShapeDtypeStruct((16, 1024), jnp.float32),
            jax.ShapeDtypeStruct((16, 1024), jnp.float32),
            jax.ShapeDtypeStruct((2, CASES, 1024), jnp.float32),
        ],
        scratch_shapes=[pltpu.VMEM((128, LANES), jnp.float32), pltpu.VMEM((2, 16, LANES), jnp.float32)],
        compiler_params=pltpu.CompilerParams(vmem_limit_bytes=8 * 2**20),
        name="finish",
    )(sums, load, image, twice, parts)


def to_all(value, axes, count):
    return lax.all_to_all(jnp.broadcast_to(value[None], (count,) + value.shape), axes, 0, 0)


def body(
    interface_load,
    schur_values,
    schur_columns,
    coupling,
    layer_inverse,
    interior_load,
    adjacency,
    live_counts,
):
    y, core, x, z = [lax.axis_index(axis) for axis in AXES]
    region = y * 2 + core
    places = locate(schur_columns, region, x, z).reshape(-1)
    slots = locate(adjacency, region, x, z).reshape(-1)
    load = interface_load.reshape(16, 8, LANES)
    matrices = prepare(schur_values)
    load_window = exchange(load)
    image = apply_first(places, load_window, matrices)
    image_window = exchange(image)
    twice, sums = apply_second(places, image_window, matrices, load, image)
    plane_sums = jnp.sum(to_all(sums, ("x", "z"), 16), axis=0)
    all_sums = to_all(plane_sums, ("y", "core"), 8)
    reduced = couple(slots, live_counts, load_window, image_window, coupling, interior_load)
    parts = layers(reduced, layer_inverse)
    return tuple(finish(all_sums, load, image, twice, parts))


def solution(mesh):
    grid = jax.sharding.Mesh(mesh.devices.reshape(SIZES), AXES)
    lead = AXES
    in_specs = (
        P(lead, None),
        P(lead, None, None),
        P(lead, None),
        P(lead, None, None),
        P(lead, None, None),
        P(lead, None, None),
        P(lead, None),
        P(lead),
    )
    out_specs = (P(lead, None), P(lead, None), P(lead, None, None))
    return jax.shard_map(body, mesh=grid, in_specs=in_specs, out_specs=out_specs, check_vma=False)
```

```python
import jax
import jax.numpy as jnp
from jax import lax
from jax.experimental import pallas as pl
from jax.experimental.pallas import tpu as pltpu
from jax.sharding import PartitionSpec as P

NB = 64
CASES = 16
LANES = 128
AXES = ("y", "core", "x", "z")
SIZES = (4, 2, 4, 4)
ORDER = (0, 1, 3, 2)
WINDOW = 768
CHIPS = 64
NT = (((1,), (1,)), ((), ()))
VMEM_SPEC = pl.BlockSpec(memory_space=pltpu.VMEM)
SMEM_SPEC = pl.BlockSpec(memory_space=pltpu.SMEM)
ANY_SPEC = pl.BlockSpec(memory_space=pl.ANY)

PLACES = [
    (y, c, x, z)
    for y in range(SIZES[0])
    for c in range(SIZES[1])
    for x in range(SIZES[2])
    for z in range(SIZES[3])
]


def flat(y, c, x, z):
    return ((y * SIZES[1] + c) * SIZES[2] + x) * SIZES[3] + z


def permute(value, target):
    pairs = []
    for place in PLACES:
        goal = target(*place)
        if goal is not None:
            pairs.append((flat(*place), flat(*goal)))
    return lax.ppermute(value, AXES, pairs)


def far(y, c, x, z):
    if c == 1:
        return (y + 1, 0, x, z) if y + 1 < SIZES[0] else None
    return (y - 1, 1, x, z) if y > 0 else None


def partner(y, c, x, z):
    return (y, 1 - c, x, z)


def along_first(step):
    return lambda y, c, x, z: (y, c, x, (z - step) % 4) if c == 0 else (y, c, (x - step) % 4, z)


def along_second(step):
    return lambda y, c, x, z: (y, c, (x - step) % 4, z) if c == 0 else (y, c, x, (z - step) % 4)


def exchange(own, beside):
    line = jnp.stack([own] + [permute(own, along_first(k)) for k in ORDER[1:]])
    near_other = permute(line, far)
    rest = jnp.stack([permute(line, along_second(k)) for k in ORDER[1:]])
    plane = jnp.concatenate([line[None], rest])
    rest_other = permute(rest, far)
    pair = permute(plane, partner)
    results = beside(rest)
    window = jnp.concatenate([plane, near_other[None], rest_other, pair])
    return window.reshape(WINDOW, 8, LANES), results


def locate(ids, region, x, z):
    goal = ids // 256
    member = ids % 256 // 16
    dx = (member // 4 - x) % 4
    dz = (member % 4 - z) % 4
    px = dx ^ (dx >> 1)
    pz = dz ^ (dz >> 1)
    place = jnp.where(goal % 2 == 1, pz * 4 + px, px * 4 + pz)
    group = jnp.where(goal == region, 0, jnp.where(goal == (region ^ 1), 2, 1))
    return (group * 16 + place) * 16 + ids % 16


def split(value):
    high = value.astype(jnp.bfloat16)
    low = (value - high.astype(jnp.float32)).astype(jnp.bfloat16)
    return high, low


def lane_ids(rows):
    return lax.broadcasted_iota(jnp.int32, (rows, LANES), 1)


def merge_halves(left, right):
    low_half = lane_ids(left.shape[0]) < NB
    first = jnp.where(low_half, left, pltpu.roll(right, NB, 1))
    second = jnp.where(low_half, pltpu.roll(left, NB, 1), right)
    return first, second


def prepare_kernel(values_ref, ready_ref, out_ref):
    lanes = lane_ids(8)
    subs = lax.broadcasted_iota(jnp.int32, (8, LANES), 0)
    for group in range(4):
        rows = []
        for pair in range(8 * group, 8 * group + 8):
            cut = slice(pair * LANES, (pair + 1) * LANES)
            upper = values_ref[0, 0:8, cut]
            lower = values_ref[0, 8:16, cut]
            own = (subs == 0) & ((lanes == 2 * pair) | (lanes == NB + 2 * pair + 1))
            upper = jnp.where(own, upper - 2.0, upper)
            rows.extend(merge_halves(upper, lower))
        tiles = jnp.transpose(jnp.stack(rows), (1, 0, 2))
        for k in range(8):
            high, low = split(tiles[k])
            out_ref[0, 16 * group : 16 * group + 16, k * LANES : (k + 1) * LANES] = high
            out_ref[0, NB + 16 * group : NB + 16 * group + 16, k * LANES : (k + 1) * LANES] = low


def prepare(values, ready):
    return pl.pallas_call(
        prepare_kernel,
        grid=(16,),
        in_specs=[pl.BlockSpec((1, 16, 4096), lambda i: (i, 0, 0)), ANY_SPEC],
        out_specs=pl.BlockSpec((1, 128, 1024), lambda i: (i, 0, 0)),
        out_shape=jax.ShapeDtypeStruct((16, 128, 1024), jnp.bfloat16),
        compiler_params=pltpu.CompilerParams(vmem_limit_bytes=8 * 2**20),
        cost_estimate=pl.CostEstimate(flops=2**24, bytes_accessed=2**23, transcendentals=0),
        name="prepare",
    )(values, ready)


def halve_kernel(
    inverse_ref, coupling_ref, load_ref, ready_ref, inverse_out_ref, coupling_out_ref, base_ref, l_ref
):
    sub = pl.program_id(0)
    size = inverse_ref.shape[1]
    rows = pl.ds(pl.multiple_of(pl.program_id(1) * size, size), size)

    @pl.when(pl.program_id(1) == 0)
    def _():
        l_ref[0:16], l_ref[16:32] = split(load_ref[0])

    coupling_out_ref[sub, 0, rows, :], coupling_out_ref[sub, 1, rows, :] = split(coupling_ref[0])
    high, low = split(inverse_ref[0])
    inverse_out_ref[sub, 0, rows, :], inverse_out_ref[sub, 1, rows, :] = high, low
    main = lax.dot_general(l_ref[...], high, NT, preferred_element_type=jnp.float32)
    rest = lax.dot_general(l_ref[0:16], low, NT, preferred_element_type=jnp.float32)
    base_ref[sub, :, rows] = main[0:16] + main[16:32] + rest


def halve(inverse, coupling, load, ready):
    cut = 256
    return pl.pallas_call(
        halve_kernel,
        grid=(2, 1024 // cut),
        in_specs=[
            pl.BlockSpec((1, cut, 1024), lambda s, n: (s, n, 0)),
            pl.BlockSpec((1, cut, 512), lambda s, n: (s, n, 0)),
            pl.BlockSpec((1, CASES, 1024), lambda s, n: (s, 0, 0)),
            ANY_SPEC,
        ],
        out_specs=[VMEM_SPEC] * 3,
        out_shape=[
            jax.ShapeDtypeStruct((2, 2, 1024, 1024), jnp.bfloat16),
            jax.ShapeDtypeStruct((2, 2, 1024, 512), jnp.bfloat16),
            jax.ShapeDtypeStruct((2, CASES, 1024), jnp.float32),
        ],
        scratch_shapes=[pltpu.VMEM((32, 1024), jnp.bfloat16)],
        compiler_params=pltpu.CompilerParams(vmem_limit_bytes=20 * 2**20),
        cost_estimate=pl.CostEstimate(flops=2**27, bytes_accessed=3 * 2**23, transcendentals=0),
        name="halve",
    )(inverse, coupling, load, ready)


def apply_rows(places_ref, window_ref, matrices_ref, x_ref, out_ref):
    low_half = lane_ids(8) < NB
    for row in range(16):
        for k in range(8):
            left = window_ref[places_ref[row * 16 + k]]
            right = window_ref[places_ref[row * 16 + k + 8]]
            high, low = split(jnp.concatenate(merge_halves(left, right)))
            x_ref[row % 2, 0:16, k * LANES : (k + 1) * LANES] = high
            x_ref[row % 2, 16:32, k * LANES : (k + 1) * LANES] = low
        product = lax.dot_general(
            x_ref[row % 2], matrices_ref[row], NT, preferred_element_type=jnp.float32
        )
        both = product[0:16] + product[16:32]
        both = both + pltpu.roll(both, NB, 1)
        out_ref[row] = jnp.where(low_half, both[0:8], both[8:16])


def pick_slots(slots_ref, live_ref, window_ref, picked_ref):
    for sub in range(2):
        for t in range(4):
            tiles = []
            for slot in (2 * t, 2 * t + 1):
                tile = window_ref[slots_ref[sub * 8 + slot]]
                tiles.append(jnp.where(slot < live_ref[sub], tile, 0.0))
            even, odd = merge_halves(*tiles)
            picked_ref[sub, t, pl.ds(0, 8, stride=2), :] = even
            picked_ref[sub, t, pl.ds(1, 8, stride=2), :] = odd


def first_kernel(
    places_ref, slots_ref, live_ref, window_ref, matrices_ref, halves_ref, image_ref, picked_ref, x_ref
):
    apply_rows(places_ref, window_ref, matrices_ref, x_ref, image_ref)
    pick_slots(slots_ref, live_ref, window_ref, picked_ref)


def second_kernel(
    places_ref,
    slots_ref,
    live_ref,
    window_ref,
    matrices_ref,
    load_ref,
    image_ref,
    folded_ref,
    twice_ref,
    sums_ref,
    parts_ref,
    x_ref,
    picked_ref,
    p_ref,
):
    apply_rows(places_ref, window_ref, matrices_ref, x_ref, twice_ref)
    load, image, twice = load_ref[...], image_ref[...], twice_ref[...]
    lanes = lane_ids(8)
    low_half = lanes < NB
    packed = jnp.zeros((8, LANES), jnp.float32)
    products = (load * load, load * image, image * image, load * twice, image * twice)
    for place, product in enumerate(products):
        tile = jnp.sum(product, axis=0)
        left = jnp.sum(jnp.where(low_half, tile, 0.0), axis=1, keepdims=True)
        right = jnp.sum(jnp.where(low_half, 0.0, tile), axis=1, keepdims=True)
        packed = jnp.where(lanes == place, left, packed)
        packed = jnp.where(lanes == NB + place, right, packed)
    sums_ref[...] = jnp.broadcast_to(packed[None], sums_ref.shape)
    pick_slots(slots_ref, live_ref, window_ref, picked_ref)
    for sub in range(2):
        for t in range(4):
            cut = slice(t * LANES, (t + 1) * LANES)
            p_ref[sub, 0:16, cut], p_ref[sub, 16:32, cut] = split(picked_ref[sub, t])
        main = lax.dot_general(p_ref[sub], folded_ref[sub, 0], NT, preferred_element_type=jnp.float32)
        rest = lax.dot_general(
            p_ref[sub, 0:16], folded_ref[sub, 1], NT, preferred_element_type=jnp.float32
        )
        parts_ref[sub] = main[0:16] + main[16:32] + rest


APPLY_COST = pl.CostEstimate(flops=2**27, bytes_accessed=2**23, transcendentals=0)
TILES = jax.ShapeDtypeStruct((16, 8, LANES), jnp.float32)
PICKED = jax.ShapeDtypeStruct((2, 4, 16, LANES), jnp.float32)


def apply_first(places, slots, live, window, matrices, halves):
    return pl.pallas_call(
        first_kernel,
        in_specs=[SMEM_SPEC] * 3 + [VMEM_SPEC] * 3,
        out_specs=[VMEM_SPEC] * 2,
        out_shape=[TILES, PICKED],
        scratch_shapes=[pltpu.VMEM((2, 32, 1024), jnp.bfloat16)],
        compiler_params=pltpu.CompilerParams(vmem_limit_bytes=6 * 2**20),
        cost_estimate=APPLY_COST,
        name="apply_first",
    )(places, slots, live, window, matrices, halves)


def apply_second(places, slots, live, window, matrices, load, image, folded):
    return pl.pallas_call(
        second_kernel,
        in_specs=[SMEM_SPEC] * 3 + [VMEM_SPEC] * 5,
        out_specs=[VMEM_SPEC] * 3,
        out_shape=[
            TILES,
            jax.ShapeDtypeStruct((CHIPS, 8, LANES), jnp.float32),
            jax.ShapeDtypeStruct((2, CASES, 1024), jnp.float32),
        ],
        scratch_shapes=[
            pltpu.VMEM((2, 32, 1024), jnp.bfloat16),
            pltpu.VMEM((2, 4, 16, LANES), jnp.float32),
            pltpu.VMEM((2, 32, 512), jnp.bfloat16),
        ],
        compiler_params=pltpu.CompilerParams(vmem_limit_bytes=8 * 2**20),
        cost_estimate=APPLY_COST,
        name="apply_second",
    )(places, slots, live, window, matrices, load, image, folded)


def fold_kernel(inverse_ref, coupling_ref, picked_ref, ready_ref, folded_ref, parts_ref, p_ref):
    cut = 256
    for sub in range(2):
        for t in range(4):
            lanes = slice(t * LANES, (t + 1) * LANES)
            p_ref[sub, 0:16, lanes], p_ref[sub, 16:32, lanes] = split(picked_ref[sub, t])

    @pl.loop(0, 2)
    def _(sub):
        for n in range(1024 // cut):
            rows = slice(n * cut, (n + 1) * cut)
            high, low = inverse_ref[sub, 0, rows], inverse_ref[sub, 1, rows]
            term = (
                jnp.dot(high, coupling_ref[sub, 0], preferred_element_type=jnp.float32)
                + jnp.dot(high, coupling_ref[sub, 1], preferred_element_type=jnp.float32)
                + jnp.dot(low, coupling_ref[sub, 0], preferred_element_type=jnp.float32)
            )
            high, low = split(term)
            folded_ref[sub, 0, rows], folded_ref[sub, 1, rows] = high, low
            main = lax.dot_general(p_ref[sub], high, NT, preferred_element_type=jnp.float32)
            rest = lax.dot_general(p_ref[sub, 0:16], low, NT, preferred_element_type=jnp.float32)
            parts_ref[sub, :, rows] = main[0:16] + main[16:32] + rest


def fold(inverse, coupling, picked, ready):
    return pl.pallas_call(
        fold_kernel,
        in_specs=[VMEM_SPEC] * 3 + [ANY_SPEC],
        out_specs=[VMEM_SPEC] * 2,
        out_shape=[
            jax.ShapeDtypeStruct((2, 2, 1024, 512), jnp.bfloat16),
            jax.ShapeDtypeStruct((2, CASES, 1024), jnp.float32),
        ],
        scratch_shapes=[pltpu.VMEM((2, 32, 512), jnp.bfloat16)],
        compiler_params=pltpu.CompilerParams(vmem_limit_bytes=10 * 2**20),
        cost_estimate=pl.CostEstimate(flops=2**33, bytes_accessed=2**24, transcendentals=0),
        name="fold",
    )(inverse, coupling, picked, ready)


def finish_kernel(
    sums_ref, others_ref, load_ref, image_ref, twice_ref, base_ref, parts_ref, more_ref, solution_ref, residual_ref, interior_ref, tiles_ref, cases_ref
):
    lanes = lane_ids(8)
    low_half = lanes < NB
    packed = sums_ref[...] + others_ref[...]

    def pick(place):
        left = jnp.sum(jnp.where(lanes == place, packed, 0.0), axis=1, keepdims=True)
        right = jnp.sum(jnp.where(lanes == NB + place, packed, 0.0), axis=1, keepdims=True)
        return jnp.where(low_half, left, right)

    uu, ue, ee, uf, ef = [pick(place) for place in range(5)]
    inner = 2.0 * uu + ue
    step = uu / inner
    along = ue / inner
    beta = step * (ee / inner) - along * along
    norm = beta * uu
    mix = along + beta
    length = mix * mix * uu - 2.0 * mix * step * ue + step * step * ee
    cross = mix * mix * ue - mix * step * (uf + ee) + step * step * ef
    last = norm / (2.0 * length + cross)
    on_load = step + last * mix
    on_image = -last * step
    rest_load = along - 2.0 * last * mix
    rest_image = -step - last * (mix - 2.0 * step)
    rest_twice = last * step

    rows = load_ref.shape[0]
    load, image, twice = load_ref[...], image_ref[...], twice_ref[...]
    for out_ref, value in (
        (solution_ref, on_load[None] * load + on_image[None] * image),
        (
            residual_ref,
            rest_load[None] * load + rest_image[None] * image + rest_twice[None] * twice,
        ),
    ):
        tiles_ref[...] = value.reshape(rows * 8, LANES)
        for s in range(8):
            out_ref[:, s * LANES : (s + 1) * LANES] = tiles_ref[pl.ds(s, rows, stride=8), :]
    for place, factor in enumerate((on_load, on_image)):
        for h in range(2):
            spread = jnp.broadcast_to(factor[:, h * NB : h * NB + 1], (8, LANES))
            cases_ref[place, pl.ds(h, 8, stride=2), :] = spread
    own, other = cases_ref[0][:, 0:1], cases_ref[1][:, 0:1]
    for sub in range(2):
        interior_ref[sub] = (
            base_ref[sub] - own * parts_ref[sub] - other * more_ref[sub]
        )


def finish(sums, others, load, image, twice, base, parts, more):
    return pl.pallas_call(
        finish_kernel,
        in_specs=[VMEM_SPEC] * 8,
        out_specs=[VMEM_SPEC] * 3,
        out_shape=[
            jax.ShapeDtypeStruct((16, 1024), jnp.float32),
            jax.ShapeDtypeStruct((16, 1024), jnp.float32),
            jax.ShapeDtypeStruct((2, CASES, 1024), jnp.float32),
        ],
        scratch_shapes=[pltpu.VMEM((128, LANES), jnp.float32), pltpu.VMEM((2, 16, LANES), jnp.float32)],
        compiler_params=pltpu.CompilerParams(vmem_limit_bytes=8 * 2**20),
        name="finish",
    )(sums, others, load, image, twice, base, parts, more)


def body(
    interface_load,
    schur_values,
    schur_columns,
    coupling,
    layer_inverse,
    interior_load,
    adjacency,
    live_counts,
):
    y, core, x, z = [lax.axis_index(axis) for axis in AXES]
    region = y * 2 + core
    places = locate(schur_columns, region, x, z).reshape(-1)
    slots = locate(adjacency, region, x, z).reshape(-1)
    load = interface_load.reshape(16, 8, LANES)
    load_window, (matrices, (inverse, couplings, base)) = exchange(
        load,
        lambda ready: (
            prepare(schur_values, ready),
            halve(layer_inverse, coupling, interior_load, ready),
        ),
    )
    image, picked = apply_first(places, slots, live_counts, load_window, matrices, inverse)
    image_window, (folded, parts) = exchange(
        image, lambda ready: fold(inverse, couplings, picked, ready)
    )
    twice, sums, more = apply_second(
        places, slots, live_counts, image_window, matrices, load, image, folded
    )
    sums = jnp.sum(lax.all_to_all(sums, ("y", "x", "z"), 0, 0), axis=0)
    return tuple(finish(sums, permute(sums, partner), load, image, twice, base, parts, more))


def solution(mesh):
    grid = jax.sharding.Mesh(mesh.devices.reshape(SIZES), AXES)
    lead = AXES
    in_specs = (
        P(lead, None),
        P(lead, None, None),
        P(lead, None),
        P(lead, None, None),
        P(lead, None, None),
        P(lead, None, None),
        P(lead, None),
        P(lead),
    )
    out_specs = (P(lead, None), P(lead, None), P(lead, None, None))
    return jax.shard_map(body, mesh=grid, in_specs=in_specs, out_specs=out_specs, check_vma=False)
```

```python
import jax
import jax.numpy as jnp
from jax import lax
from jax.experimental import pallas as pl
from jax.experimental.pallas import tpu as pltpu
from jax.sharding import PartitionSpec as P

NB = 64
CASES = 16
LANES = 128
AXES = ("y", "core", "x", "z")
SIZES = (4, 2, 4, 4)
ORDER = (0, 1, 3, 2)
WINDOW = 768
CHIPS = 64
NT = (((1,), (1,)), ((), ()))
VMEM_SPEC = pl.BlockSpec(memory_space=pltpu.VMEM)
SMEM_SPEC = pl.BlockSpec(memory_space=pltpu.SMEM)
ANY_SPEC = pl.BlockSpec(memory_space=pl.ANY)

PLACES = [
    (y, c, x, z)
    for y in range(SIZES[0])
    for c in range(SIZES[1])
    for x in range(SIZES[2])
    for z in range(SIZES[3])
]


def flat(y, c, x, z):
    return ((y * SIZES[1] + c) * SIZES[2] + x) * SIZES[3] + z


def permute(value, target):
    pairs = []
    for place in PLACES:
        goal = target(*place)
        if goal is not None:
            pairs.append((flat(*place), flat(*goal)))
    return lax.ppermute(value, AXES, pairs)


def far(y, c, x, z):
    if c == 1:
        return (y + 1, 0, x, z) if y + 1 < SIZES[0] else None
    return (y - 1, 1, x, z) if y > 0 else None


def partner(y, c, x, z):
    return (y, 1 - c, x, z)


def along_first(step):
    return lambda y, c, x, z: (y, c, x, (z - step) % 4) if c == 0 else (y, c, (x - step) % 4, z)


def along_second(step):
    return lambda y, c, x, z: (y, c, (x - step) % 4, z) if c == 0 else (y, c, x, (z - step) % 4)


def exchange(own, beside):
    line = jnp.stack([own] + [permute(own, along_first(k)) for k in ORDER[1:]])
    near_other = permute(line, far)
    rest = jnp.stack([permute(line, along_second(k)) for k in ORDER[1:]])
    plane = jnp.concatenate([line[None], rest])
    rest_other = permute(rest, far)
    pair = permute(plane, partner)
    results = beside(rest)
    window = jnp.concatenate([plane, near_other[None], rest_other, pair])
    return window.reshape(WINDOW, 8, LANES), results


def locate(ids, region, x, z):
    goal = ids // 256
    member = ids % 256 // 16
    dx = (member // 4 - x) % 4
    dz = (member % 4 - z) % 4
    px = dx ^ (dx >> 1)
    pz = dz ^ (dz >> 1)
    place = jnp.where(goal % 2 == 1, pz * 4 + px, px * 4 + pz)
    group = jnp.where(goal == region, 0, jnp.where(goal == (region ^ 1), 2, 1))
    return (group * 16 + place) * 16 + ids % 16


def split(value):
    high = value.astype(jnp.bfloat16)
    low = (value - high.astype(jnp.float32)).astype(jnp.bfloat16)
    return high, low


def lane_ids(rows):
    return lax.broadcasted_iota(jnp.int32, (rows, LANES), 1)


def merge_halves(left, right):
    low_half = lane_ids(left.shape[0]) < NB
    first = jnp.where(low_half, left, pltpu.roll(right, NB, 1))
    second = jnp.where(low_half, pltpu.roll(left, NB, 1), right)
    return first, second


def prepare_kernel(values_ref, ready_ref, out_ref):
    lanes = lane_ids(8)
    subs = lax.broadcasted_iota(jnp.int32, (8, LANES), 0)
    for group in range(4):
        rows = []
        for pair in range(8 * group, 8 * group + 8):
            cut = slice(pair * LANES, (pair + 1) * LANES)
            upper = values_ref[0, 0:8, cut]
            lower = values_ref[0, 8:16, cut]
            own = (subs == 0) & ((lanes == 2 * pair) | (lanes == NB + 2 * pair + 1))
            upper = jnp.where(own, upper - 2.0, upper)
            rows.extend(merge_halves(upper, lower))
        tiles = jnp.transpose(jnp.stack(rows), (1, 0, 2))
        for k in range(8):
            high, low = split(tiles[k])
            out_ref[0, 16 * group : 16 * group + 16, k * LANES : (k + 1) * LANES] = high
            out_ref[0, NB + 16 * group : NB + 16 * group + 16, k * LANES : (k + 1) * LANES] = low


def prepare(values, ready):
    return pl.pallas_call(
        prepare_kernel,
        grid=(16,),
        in_specs=[pl.BlockSpec((1, 16, 4096), lambda i: (i, 0, 0)), ANY_SPEC],
        out_specs=pl.BlockSpec((1, 128, 1024), lambda i: (i, 0, 0)),
        out_shape=jax.ShapeDtypeStruct((16, 128, 1024), jnp.bfloat16),
        compiler_params=pltpu.CompilerParams(vmem_limit_bytes=8 * 2**20),
        cost_estimate=pl.CostEstimate(flops=2**24, bytes_accessed=2**23, transcendentals=0),
        name="prepare",
    )(values, ready)


def halve_kernel(inverse_ref, coupling_ref, ready_ref, inverse_out_ref, coupling_out_ref):
    sub = pl.program_id(0)
    size = inverse_ref.shape[1]
    rows = pl.ds(pl.multiple_of(pl.program_id(1) * size, size), size)
    for ref, out_ref in ((inverse_ref, inverse_out_ref), (coupling_ref, coupling_out_ref)):
        out_ref[sub, 0, rows, :], out_ref[sub, 1, rows, :] = split(ref[0])


def halve(inverse, coupling, ready):
    cut = 256
    return pl.pallas_call(
        halve_kernel,
        grid=(2, 1024 // cut),
        in_specs=[
            pl.BlockSpec((1, cut, 1024), lambda s, n: (s, n, 0)),
            pl.BlockSpec((1, cut, 512), lambda s, n: (s, n, 0)),
            ANY_SPEC,
        ],
        out_specs=[VMEM_SPEC] * 2,
        out_shape=[
            jax.ShapeDtypeStruct((2, 2, 1024, 1024), jnp.bfloat16),
            jax.ShapeDtypeStruct((2, 2, 1024, 512), jnp.bfloat16),
        ],
        compiler_params=pltpu.CompilerParams(vmem_limit_bytes=20 * 2**20),
        cost_estimate=pl.CostEstimate(flops=2**24, bytes_accessed=3 * 2**23, transcendentals=0),
        name="halve",
    )(inverse, coupling, ready)


def apply_rows(places_ref, window_ref, matrices_ref, x_ref, out_ref):
    low_half = lane_ids(8) < NB
    for row in range(16):
        for k in range(8):
            left = window_ref[places_ref[row * 16 + k]]
            right = window_ref[places_ref[row * 16 + k + 8]]
            high, low = split(jnp.concatenate(merge_halves(left, right)))
            x_ref[row % 2, 0:16, k * LANES : (k + 1) * LANES] = high
            x_ref[row % 2, 16:32, k * LANES : (k + 1) * LANES] = low
        product = lax.dot_general(
            x_ref[row % 2], matrices_ref[row], NT, preferred_element_type=jnp.float32
        )
        both = product[0:16] + product[16:32]
        both = both + pltpu.roll(both, NB, 1)
        out_ref[row] = jnp.where(low_half, both[0:8], both[8:16])


def pick_slots(slots_ref, live_ref, window_ref, picked_ref):
    for sub in range(2):
        for t in range(4):
            tiles = []
            for slot in (2 * t, 2 * t + 1):
                tile = window_ref[slots_ref[sub * 8 + slot]]
                tiles.append(jnp.where(slot < live_ref[sub], tile, 0.0))
            even, odd = merge_halves(*tiles)
            picked_ref[sub, t, pl.ds(0, 8, stride=2), :] = even
            picked_ref[sub, t, pl.ds(1, 8, stride=2), :] = odd


def first_kernel(
    places_ref, slots_ref, live_ref, window_ref, matrices_ref, halves_ref, image_ref, picked_ref, x_ref
):
    apply_rows(places_ref, window_ref, matrices_ref, x_ref, image_ref)
    pick_slots(slots_ref, live_ref, window_ref, picked_ref)


def second_kernel(
    places_ref,
    slots_ref,
    live_ref,
    window_ref,
    matrices_ref,
    load_ref,
    image_ref,
    folded_ref,
    first_ref,
    twice_ref,
    sums_ref,
    parts_ref,
    x_ref,
    picked_ref,
    p_ref,
):
    apply_rows(places_ref, window_ref, matrices_ref, x_ref, twice_ref)
    load, image, twice = load_ref[...], image_ref[...], twice_ref[...]
    lanes = lane_ids(8)
    low_half = lanes < NB
    packed = jnp.zeros((8, LANES), jnp.float32)
    products = (load * load, load * image, image * image, load * twice, image * twice)
    for place, product in enumerate(products):
        tile = jnp.sum(product, axis=0)
        left = jnp.sum(jnp.where(low_half, tile, 0.0), axis=1, keepdims=True)
        right = jnp.sum(jnp.where(low_half, 0.0, tile), axis=1, keepdims=True)
        packed = jnp.where(lanes == place, left, packed)
        packed = jnp.where(lanes == NB + place, right, packed)
    sums_ref[...] = jnp.broadcast_to(packed[None], sums_ref.shape)
    pick_slots(slots_ref, live_ref, window_ref, picked_ref)
    for sub in range(2):
        for which, ref in enumerate((first_ref, picked_ref)):
            for t in range(4):
                cut = slice(t * LANES, (t + 1) * LANES)
                high, low = split(ref[sub, t])
                p_ref[sub, 16 * which : 16 * which + 16, cut] = high
                p_ref[sub, 32 + 16 * which : 48 + 16 * which, cut] = low
        main = lax.dot_general(p_ref[sub], folded_ref[sub, 0], NT, preferred_element_type=jnp.float32)
        rest = lax.dot_general(
            p_ref[sub, 0:32], folded_ref[sub, 1], NT, preferred_element_type=jnp.float32
        )
        parts_ref[sub] = main[0:32] + main[32:64] + rest


APPLY_COST = pl.CostEstimate(flops=2**27, bytes_accessed=2**23, transcendentals=0)
TILES = jax.ShapeDtypeStruct((16, 8, LANES), jnp.float32)
PICKED = jax.ShapeDtypeStruct((2, 4, 16, LANES), jnp.float32)


def apply_first(places, slots, live, window, matrices, halves):
    return pl.pallas_call(
        first_kernel,
        in_specs=[SMEM_SPEC] * 3 + [VMEM_SPEC] * 3,
        out_specs=[VMEM_SPEC] * 2,
        out_shape=[TILES, PICKED],
        scratch_shapes=[pltpu.VMEM((2, 32, 1024), jnp.bfloat16)],
        compiler_params=pltpu.CompilerParams(vmem_limit_bytes=6 * 2**20),
        cost_estimate=APPLY_COST,
        name="apply_first",
    )(places, slots, live, window, matrices, halves)


def apply_second(places, slots, live, window, matrices, load, image, folded, first):
    return pl.pallas_call(
        second_kernel,
        in_specs=[SMEM_SPEC] * 3 + [VMEM_SPEC] * 6,
        out_specs=[VMEM_SPEC] * 3,
        out_shape=[
            TILES,
            jax.ShapeDtypeStruct((CHIPS, 8, LANES), jnp.float32),
            jax.ShapeDtypeStruct((2, 32, 1024), jnp.float32),
        ],
        scratch_shapes=[
            pltpu.VMEM((2, 32, 1024), jnp.bfloat16),
            pltpu.VMEM((2, 4, 16, LANES), jnp.float32),
            pltpu.VMEM((2, 64, 512), jnp.bfloat16),
        ],
        compiler_params=pltpu.CompilerParams(vmem_limit_bytes=8 * 2**20),
        cost_estimate=APPLY_COST,
        name="apply_second",
    )(places, slots, live, window, matrices, load, image, folded, first)


def fold_kernel(inverse_ref, coupling_ref, load_ref, ready_ref, folded_ref, base_ref, l_ref):
    cut = 256
    for sub in range(2):
        l_ref[sub, 0:16], l_ref[sub, 16:32] = split(load_ref[sub])

    @pl.loop(0, 2)
    def _(sub):
        for n in range(1024 // cut):
            rows = slice(n * cut, (n + 1) * cut)
            high, low = inverse_ref[sub, 0, rows], inverse_ref[sub, 1, rows]
            folded_ref[sub, 0, rows], folded_ref[sub, 1, rows] = split(
                jnp.dot(high, coupling_ref[sub, 0], preferred_element_type=jnp.float32)
                + jnp.dot(high, coupling_ref[sub, 1], preferred_element_type=jnp.float32)
                + jnp.dot(low, coupling_ref[sub, 0], preferred_element_type=jnp.float32)
            )
            main = lax.dot_general(l_ref[sub], high, NT, preferred_element_type=jnp.float32)
            rest = lax.dot_general(l_ref[sub, 0:16], low, NT, preferred_element_type=jnp.float32)
            base_ref[sub, :, rows] = main[0:16] + main[16:32] + rest


def fold(inverse, coupling, load, ready):
    return pl.pallas_call(
        fold_kernel,
        in_specs=[VMEM_SPEC] * 3 + [ANY_SPEC],
        out_specs=[VMEM_SPEC] * 2,
        out_shape=[
            jax.ShapeDtypeStruct((2, 2, 1024, 512), jnp.bfloat16),
            jax.ShapeDtypeStruct((2, CASES, 1024), jnp.float32),
        ],
        scratch_shapes=[pltpu.VMEM((2, 32, 1024), jnp.bfloat16)],
        compiler_params=pltpu.CompilerParams(vmem_limit_bytes=10 * 2**20),
        cost_estimate=pl.CostEstimate(flops=2**33, bytes_accessed=2**24, transcendentals=0),
        name="fold",
    )(inverse, coupling, load, ready)


def finish_kernel(
    sums_ref, others_ref, load_ref, image_ref, twice_ref, base_ref, parts_ref, solution_ref, residual_ref, interior_ref, tiles_ref, cases_ref
):
    lanes = lane_ids(8)
    low_half = lanes < NB
    packed = sums_ref[...] + others_ref[...]

    def pick(place):
        left = jnp.sum(jnp.where(lanes == place, packed, 0.0), axis=1, keepdims=True)
        right = jnp.sum(jnp.where(lanes == NB + place, packed, 0.0), axis=1, keepdims=True)
        return jnp.where(low_half, left, right)

    uu, ue, ee, uf, ef = [pick(place) for place in range(5)]
    inner = 2.0 * uu + ue
    step = uu / inner
    along = ue / inner
    beta = step * (ee / inner) - along * along
    norm = beta * uu
    mix = along + beta
    length = mix * mix * uu - 2.0 * mix * step * ue + step * step * ee
    cross = mix * mix * ue - mix * step * (uf + ee) + step * step * ef
    last = norm / (2.0 * length + cross)
    on_load = step + last * mix
    on_image = -last * step
    rest_load = along - 2.0 * last * mix
    rest_image = -step - last * (mix - 2.0 * step)
    rest_twice = last * step

    rows = load_ref.shape[0]
    load, image, twice = load_ref[...], image_ref[...], twice_ref[...]
    for out_ref, value in (
        (solution_ref, on_load[None] * load + on_image[None] * image),
        (
            residual_ref,
            rest_load[None] * load + rest_image[None] * image + rest_twice[None] * twice,
        ),
    ):
        tiles_ref[...] = value.reshape(rows * 8, LANES)
        for s in range(8):
            out_ref[:, s * LANES : (s + 1) * LANES] = tiles_ref[pl.ds(s, rows, stride=8), :]
    for place, factor in enumerate((on_load, on_image)):
        for h in range(2):
            spread = jnp.broadcast_to(factor[:, h * NB : h * NB + 1], (8, LANES))
            cases_ref[place, pl.ds(h, 8, stride=2), :] = spread
    own, other = cases_ref[0][:, 0:1], cases_ref[1][:, 0:1]
    for sub in range(2):
        interior_ref[sub] = (
            base_ref[sub] - own * parts_ref[sub, 0:16] - other * parts_ref[sub, 16:32]
        )


def finish(sums, others, load, image, twice, base, parts):
    return pl.pallas_call(
        finish_kernel,
        in_specs=[VMEM_SPEC] * 7,
        out_specs=[VMEM_SPEC] * 3,
        out_shape=[
            jax.ShapeDtypeStruct((16, 1024), jnp.float32),
            jax.ShapeDtypeStruct((16, 1024), jnp.float32),
            jax.ShapeDtypeStruct((2, CASES, 1024), jnp.float32),
        ],
        scratch_shapes=[pltpu.VMEM((128, LANES), jnp.float32), pltpu.VMEM((2, 16, LANES), jnp.float32)],
        compiler_params=pltpu.CompilerParams(vmem_limit_bytes=8 * 2**20),
        name="finish",
    )(sums, others, load, image, twice, base, parts)


def body(
    interface_load,
    schur_values,
    schur_columns,
    coupling,
    layer_inverse,
    interior_load,
    adjacency,
    live_counts,
):
    y, core, x, z = [lax.axis_index(axis) for axis in AXES]
    region = y * 2 + core
    places = locate(schur_columns, region, x, z).reshape(-1)
    slots = locate(adjacency, region, x, z).reshape(-1)
    load = interface_load.reshape(16, 8, LANES)
    load_window, (matrices, (inverse, couplings)) = exchange(
        load, lambda ready: (prepare(schur_values, ready), halve(layer_inverse, coupling, ready))
    )
    image, picked = apply_first(places, slots, live_counts, load_window, matrices, inverse)
    image_window, (folded, base) = exchange(
        image, lambda ready: fold(inverse, couplings, interior_load, ready)
    )
    twice, sums, parts = apply_second(
        places, slots, live_counts, image_window, matrices, load, image, folded, picked
    )
    sums = jnp.sum(lax.all_to_all(sums, ("y", "x", "z"), 0, 0), axis=0)
    return tuple(finish(sums, permute(sums, partner), load, image, twice, base, parts))


def solution(mesh):
    grid = jax.sharding.Mesh(mesh.devices.reshape(SIZES), AXES)
    lead = AXES
    in_specs = (
        P(lead, None),
        P(lead, None, None),
        P(lead, None),
        P(lead, None, None),
        P(lead, None, None),
        P(lead, None, None),
        P(lead, None),
        P(lead),
    )
    out_specs = (P(lead, None), P(lead, None), P(lead, None, None))
    return jax.shard_map(body, mesh=grid, in_specs=in_specs, out_specs=out_specs, check_vma=False)
```

```python
import jax
import jax.numpy as jnp
from jax import lax
from jax.experimental import pallas as pl
from jax.experimental.pallas import tpu as pltpu
from jax.sharding import PartitionSpec as P

NB = 64
CASES = 16
LANES = 128
AXES = ("y", "core", "x", "z")
SIZES = (4, 2, 4, 4)
ORDER = (0, 1, 3, 2)
WINDOW = 768
CHIPS = 64
NT = (((1,), (1,)), ((), ()))
VMEM_SPEC = pl.BlockSpec(memory_space=pltpu.VMEM)
SMEM_SPEC = pl.BlockSpec(memory_space=pltpu.SMEM)
ANY_SPEC = pl.BlockSpec(memory_space=pl.ANY)

PLACES = [
    (y, c, x, z)
    for y in range(SIZES[0])
    for c in range(SIZES[1])
    for x in range(SIZES[2])
    for z in range(SIZES[3])
]


def flat(y, c, x, z):
    return ((y * SIZES[1] + c) * SIZES[2] + x) * SIZES[3] + z


def permute(value, target):
    pairs = []
    for place in PLACES:
        goal = target(*place)
        if goal is not None:
            pairs.append((flat(*place), flat(*goal)))
    return lax.ppermute(value, AXES, pairs)


def far(y, c, x, z):
    if c == 1:
        return (y + 1, 0, x, z) if y + 1 < SIZES[0] else None
    return (y - 1, 1, x, z) if y > 0 else None


def partner(y, c, x, z):
    return (y, 1 - c, x, z)


def along_first(step):
    return lambda y, c, x, z: (y, c, x, (z - step) % 4) if c == 0 else (y, c, (x - step) % 4, z)


def along_second(step):
    return lambda y, c, x, z: (y, c, (x - step) % 4, z) if c == 0 else (y, c, x, (z - step) % 4)


def exchange(own, beside):
    line = jnp.stack([own] + [permute(own, along_first(k)) for k in ORDER[1:]])
    near_other = permute(line, far)
    rest = jnp.stack([permute(line, along_second(k)) for k in ORDER[1:]])
    plane = jnp.concatenate([line[None], rest])
    rest_other = permute(rest, far)
    pair = permute(plane, partner)
    results = beside(rest)
    window = jnp.concatenate([plane, near_other[None], rest_other, pair])
    return window.reshape(WINDOW, 8, LANES), results


def locate(ids, region, x, z):
    goal = ids // 256
    member = ids % 256 // 16
    dx = (member // 4 - x) % 4
    dz = (member % 4 - z) % 4
    px = dx ^ (dx >> 1)
    pz = dz ^ (dz >> 1)
    place = jnp.where(goal % 2 == 1, pz * 4 + px, px * 4 + pz)
    group = jnp.where(goal == region, 0, jnp.where(goal == (region ^ 1), 2, 1))
    return (group * 16 + place) * 16 + ids % 16


def split(value):
    high = value.astype(jnp.bfloat16)
    low = (value - high.astype(jnp.float32)).astype(jnp.bfloat16)
    return high, low


def times(rows, high, low):
    count = rows.shape[0]
    top, bottom = split(rows)
    main = lax.dot_general(
        jnp.concatenate([top, bottom]), high, NT, preferred_element_type=jnp.float32
    )
    rest = lax.dot_general(top, low, NT, preferred_element_type=jnp.float32)
    return main[:count] + main[count:] + rest


def lane_ids(rows):
    return lax.broadcasted_iota(jnp.int32, (rows, LANES), 1)


def merge_halves(left, right):
    low_half = lane_ids(left.shape[0]) < NB
    first = jnp.where(low_half, left, pltpu.roll(right, NB, 1))
    second = jnp.where(low_half, pltpu.roll(left, NB, 1), right)
    return first, second


def prepare_kernel(values_ref, ready_ref, out_ref):
    lanes = lane_ids(8)
    subs = lax.broadcasted_iota(jnp.int32, (8, LANES), 0)
    for group in range(4):
        rows = []
        for pair in range(8 * group, 8 * group + 8):
            cut = slice(pair * LANES, (pair + 1) * LANES)
            upper = values_ref[0, 0:8, cut]
            lower = values_ref[0, 8:16, cut]
            own = (subs == 0) & ((lanes == 2 * pair) | (lanes == NB + 2 * pair + 1))
            upper = jnp.where(own, upper - 2.0, upper)
            rows.extend(merge_halves(upper, lower))
        tiles = jnp.transpose(jnp.stack(rows), (1, 0, 2))
        for k in range(8):
            high, low = split(tiles[k])
            out_ref[0, 16 * group : 16 * group + 16, k * LANES : (k + 1) * LANES] = high
            out_ref[0, NB + 16 * group : NB + 16 * group + 16, k * LANES : (k + 1) * LANES] = low


def prepare(values, ready):
    return pl.pallas_call(
        prepare_kernel,
        grid=(16,),
        in_specs=[pl.BlockSpec((1, 16, 4096), lambda i: (i, 0, 0)), ANY_SPEC],
        out_specs=pl.BlockSpec((1, 128, 1024), lambda i: (i, 0, 0)),
        out_shape=jax.ShapeDtypeStruct((16, 128, 1024), jnp.bfloat16),
        compiler_params=pltpu.CompilerParams(vmem_limit_bytes=8 * 2**20),
        cost_estimate=pl.CostEstimate(flops=2**24, bytes_accessed=2**23, transcendentals=0),
        name="prepare",
    )(values, ready)


def halve_kernel(
    inverse_ref, coupling_ref, load_ref, ready_ref, inverse_out_ref, coupling_out_ref, base_ref
):
    sub = pl.program_id(0)
    size = inverse_ref.shape[1]
    rows = pl.ds(pl.multiple_of(pl.program_id(1) * size, size), size)
    for ref, out_ref in ((inverse_ref, inverse_out_ref), (coupling_ref, coupling_out_ref)):
        out_ref[sub, 0, rows, :], out_ref[sub, 1, rows, :] = split(ref[0])

    @pl.when(sub == 0)
    def _():
        base_ref[:, rows] = times(load_ref[0], *split(inverse_ref[0]))


def halve(inverse, coupling, load, ready):
    cut = 256
    return pl.pallas_call(
        halve_kernel,
        grid=(2, 1024 // cut),
        in_specs=[
            pl.BlockSpec((1, cut, 1024), lambda s, n: (s, n, 0)),
            pl.BlockSpec((1, cut, 512), lambda s, n: (s, n, 0)),
            VMEM_SPEC,
            ANY_SPEC,
        ],
        out_specs=[VMEM_SPEC] * 3,
        out_shape=[
            jax.ShapeDtypeStruct((2, 2, 1024, 1024), jnp.bfloat16),
            jax.ShapeDtypeStruct((2, 2, 1024, 512), jnp.bfloat16),
            jax.ShapeDtypeStruct((CASES, 1024), jnp.float32),
        ],
        compiler_params=pltpu.CompilerParams(vmem_limit_bytes=20 * 2**20),
        cost_estimate=pl.CostEstimate(flops=2**24, bytes_accessed=3 * 2**23, transcendentals=0),
        name="halve",
    )(inverse, coupling, load, ready)


def apply_rows(places_ref, window_ref, matrices_ref, x_ref, out_ref):
    low_half = lane_ids(8) < NB
    for row in range(16):
        for k in range(8):
            left = window_ref[places_ref[row * 16 + k]]
            right = window_ref[places_ref[row * 16 + k + 8]]
            high, low = split(jnp.concatenate(merge_halves(left, right)))
            x_ref[row % 2, 0:16, k * LANES : (k + 1) * LANES] = high
            x_ref[row % 2, 16:32, k * LANES : (k + 1) * LANES] = low
        product = lax.dot_general(
            x_ref[row % 2], matrices_ref[row], NT, preferred_element_type=jnp.float32
        )
        both = product[0:16] + product[16:32]
        both = both + pltpu.roll(both, NB, 1)
        out_ref[row] = jnp.where(low_half, both[0:8], both[8:16])


def pick_slots(slots_ref, live_ref, window_ref, picked_ref):
    for sub in range(2):
        for t in range(4):
            tiles = []
            for slot in (2 * t, 2 * t + 1):
                tile = window_ref[slots_ref[sub * 8 + slot]]
                tiles.append(jnp.where(slot < live_ref[sub], tile, 0.0))
            even, odd = merge_halves(*tiles)
            picked_ref[sub, t, pl.ds(0, 8, stride=2), :] = even
            picked_ref[sub, t, pl.ds(1, 8, stride=2), :] = odd


def first_kernel(
    places_ref, slots_ref, live_ref, window_ref, matrices_ref, halves_ref, image_ref, picked_ref, x_ref
):
    apply_rows(places_ref, window_ref, matrices_ref, x_ref, image_ref)
    pick_slots(slots_ref, live_ref, window_ref, picked_ref)


def second_kernel(
    places_ref,
    slots_ref,
    live_ref,
    window_ref,
    matrices_ref,
    load_ref,
    image_ref,
    folded_ref,
    first_ref,
    twice_ref,
    sums_ref,
    parts_ref,
    x_ref,
    picked_ref,
    p_ref,
):
    apply_rows(places_ref, window_ref, matrices_ref, x_ref, twice_ref)
    load, image, twice = load_ref[...], image_ref[...], twice_ref[...]
    lanes = lane_ids(8)
    low_half = lanes < NB
    packed = jnp.zeros((8, LANES), jnp.float32)
    products = (load * load, load * image, image * image, load * twice, image * twice)
    for place, product in enumerate(products):
        tile = jnp.sum(product, axis=0)
        left = jnp.sum(jnp.where(low_half, tile, 0.0), axis=1, keepdims=True)
        right = jnp.sum(jnp.where(low_half, 0.0, tile), axis=1, keepdims=True)
        packed = jnp.where(lanes == place, left, packed)
        packed = jnp.where(lanes == NB + place, right, packed)
    sums_ref[...] = jnp.broadcast_to(packed[None], sums_ref.shape)
    pick_slots(slots_ref, live_ref, window_ref, picked_ref)
    for sub in range(2):
        for which, ref in enumerate((first_ref, picked_ref)):
            for t in range(4):
                cut = slice(t * LANES, (t + 1) * LANES)
                high, low = split(ref[sub, t])
                p_ref[sub, 16 * which : 16 * which + 16, cut] = high
                p_ref[sub, 32 + 16 * which : 48 + 16 * which, cut] = low
        main = lax.dot_general(p_ref[sub], folded_ref[sub, 0], NT, preferred_element_type=jnp.float32)
        rest = lax.dot_general(
            p_ref[sub, 0:32], folded_ref[sub, 1], NT, preferred_element_type=jnp.float32
        )
        parts_ref[sub] = main[0:32] + main[32:64] + rest


APPLY_COST = pl.CostEstimate(flops=2**27, bytes_accessed=2**23, transcendentals=0)
TILES = jax.ShapeDtypeStruct((16, 8, LANES), jnp.float32)
PICKED = jax.ShapeDtypeStruct((2, 4, 16, LANES), jnp.float32)


def apply_first(places, slots, live, window, matrices, halves):
    return pl.pallas_call(
        first_kernel,
        in_specs=[SMEM_SPEC] * 3 + [VMEM_SPEC] * 3,
        out_specs=[VMEM_SPEC] * 2,
        out_shape=[TILES, PICKED],
        scratch_shapes=[pltpu.VMEM((2, 32, 1024), jnp.bfloat16)],
        compiler_params=pltpu.CompilerParams(vmem_limit_bytes=6 * 2**20),
        cost_estimate=APPLY_COST,
        name="apply_first",
    )(places, slots, live, window, matrices, halves)


def apply_second(places, slots, live, window, matrices, load, image, folded, first):
    return pl.pallas_call(
        second_kernel,
        in_specs=[SMEM_SPEC] * 3 + [VMEM_SPEC] * 6,
        out_specs=[VMEM_SPEC] * 3,
        out_shape=[
            TILES,
            jax.ShapeDtypeStruct((CHIPS, 8, LANES), jnp.float32),
            jax.ShapeDtypeStruct((2, 32, 1024), jnp.float32),
        ],
        scratch_shapes=[
            pltpu.VMEM((2, 32, 1024), jnp.bfloat16),
            pltpu.VMEM((2, 4, 16, LANES), jnp.float32),
            pltpu.VMEM((2, 64, 512), jnp.bfloat16),
        ],
        compiler_params=pltpu.CompilerParams(vmem_limit_bytes=8 * 2**20),
        cost_estimate=APPLY_COST,
        name="apply_second",
    )(places, slots, live, window, matrices, load, image, folded, first)


def fold_kernel(inverse_ref, coupling_ref, load_ref, ready_ref, folded_ref, base_ref):
    cut = 256
    base_ref[...] = times(load_ref[1], inverse_ref[1, 0], inverse_ref[1, 1])

    @pl.loop(0, 2)
    def _(sub):
        for n in range(1024 // cut):
            rows = slice(n * cut, (n + 1) * cut)
            high, low = inverse_ref[sub, 0, rows], inverse_ref[sub, 1, rows]
            folded_ref[sub, 0, rows], folded_ref[sub, 1, rows] = split(
                jnp.dot(high, coupling_ref[sub, 0], preferred_element_type=jnp.float32)
                + jnp.dot(high, coupling_ref[sub, 1], preferred_element_type=jnp.float32)
                + jnp.dot(low, coupling_ref[sub, 0], preferred_element_type=jnp.float32)
            )


def fold(inverse, coupling, load, ready):
    return pl.pallas_call(
        fold_kernel,
        in_specs=[VMEM_SPEC] * 3 + [ANY_SPEC],
        out_specs=[VMEM_SPEC] * 2,
        out_shape=[
            jax.ShapeDtypeStruct((2, 2, 1024, 512), jnp.bfloat16),
            jax.ShapeDtypeStruct((CASES, 1024), jnp.float32),
        ],
        compiler_params=pltpu.CompilerParams(vmem_limit_bytes=10 * 2**20),
        cost_estimate=pl.CostEstimate(flops=2**33, bytes_accessed=2**24, transcendentals=0),
        name="fold",
    )(inverse, coupling, load, ready)


def finish_kernel(
    sums_ref, others_ref, load_ref, image_ref, twice_ref, base0_ref, base1_ref, parts_ref, solution_ref, residual_ref, interior_ref, tiles_ref, cases_ref
):
    lanes = lane_ids(8)
    low_half = lanes < NB
    packed = sums_ref[...] + others_ref[...]

    def pick(place):
        left = jnp.sum(jnp.where(lanes == place, packed, 0.0), axis=1, keepdims=True)
        right = jnp.sum(jnp.where(lanes == NB + place, packed, 0.0), axis=1, keepdims=True)
        return jnp.where(low_half, left, right)

    uu, ue, ee, uf, ef = [pick(place) for place in range(5)]
    inner = 2.0 * uu + ue
    step = uu / inner
    along = ue / inner
    beta = step * (ee / inner) - along * along
    norm = beta * uu
    mix = along + beta
    length = mix * mix * uu - 2.0 * mix * step * ue + step * step * ee
    cross = mix * mix * ue - mix * step * (uf + ee) + step * step * ef
    last = norm / (2.0 * length + cross)
    on_load = step + last * mix
    on_image = -last * step
    rest_load = along - 2.0 * last * mix
    rest_image = -step - last * (mix - 2.0 * step)
    rest_twice = last * step

    rows = load_ref.shape[0]
    load, image, twice = load_ref[...], image_ref[...], twice_ref[...]
    for out_ref, value in (
        (solution_ref, on_load[None] * load + on_image[None] * image),
        (
            residual_ref,
            rest_load[None] * load + rest_image[None] * image + rest_twice[None] * twice,
        ),
    ):
        tiles_ref[...] = value.reshape(rows * 8, LANES)
        for s in range(8):
            out_ref[:, s * LANES : (s + 1) * LANES] = tiles_ref[pl.ds(s, rows, stride=8), :]
    for place, factor in enumerate((on_load, on_image)):
        for h in range(2):
            spread = jnp.broadcast_to(factor[:, h * NB : h * NB + 1], (8, LANES))
            cases_ref[place, pl.ds(h, 8, stride=2), :] = spread
    own, other = cases_ref[0][:, 0:1], cases_ref[1][:, 0:1]
    for sub, base_ref in enumerate((base0_ref, base1_ref)):
        interior_ref[sub] = (
            base_ref[...] - own * parts_ref[sub, 0:16] - other * parts_ref[sub, 16:32]
        )


def finish(sums, others, load, image, twice, base0, base1, parts):
    return pl.pallas_call(
        finish_kernel,
        in_specs=[VMEM_SPEC] * 8,
        out_specs=[VMEM_SPEC] * 3,
        out_shape=[
            jax.ShapeDtypeStruct((16, 1024), jnp.float32),
            jax.ShapeDtypeStruct((16, 1024), jnp.float32),
            jax.ShapeDtypeStruct((2, CASES, 1024), jnp.float32),
        ],
        scratch_shapes=[pltpu.VMEM((128, LANES), jnp.float32), pltpu.VMEM((2, 16, LANES), jnp.float32)],
        compiler_params=pltpu.CompilerParams(vmem_limit_bytes=8 * 2**20),
        name="finish",
    )(sums, others, load, image, twice, base0, base1, parts)


def body(
    interface_load,
    schur_values,
    schur_columns,
    coupling,
    layer_inverse,
    interior_load,
    adjacency,
    live_counts,
):
    y, core, x, z = [lax.axis_index(axis) for axis in AXES]
    region = y * 2 + core
    places = locate(schur_columns, region, x, z).reshape(-1)
    slots = locate(adjacency, region, x, z).reshape(-1)
    load = interface_load.reshape(16, 8, LANES)
    load_window, (matrices, (inverse, couplings, base0)) = exchange(
        load,
        lambda ready: (
            prepare(schur_values, ready),
            halve(layer_inverse, coupling, interior_load, ready),
        ),
    )
    image, picked = apply_first(places, slots, live_counts, load_window, matrices, inverse)
    image_window, (folded, base1) = exchange(
        image, lambda ready: fold(inverse, couplings, interior_load, ready)
    )
    twice, sums, parts = apply_second(
        places, slots, live_counts, image_window, matrices, load, image, folded, picked
    )
    sums = jnp.sum(lax.all_to_all(sums, ("y", "x", "z"), 0, 0), axis=0)
    return tuple(finish(sums, permute(sums, partner), load, image, twice, base0, base1, parts))


def solution(mesh):
    grid = jax.sharding.Mesh(mesh.devices.reshape(SIZES), AXES)
    lead = AXES
    in_specs = (
        P(lead, None),
        P(lead, None, None),
        P(lead, None),
        P(lead, None, None),
        P(lead, None, None),
        P(lead, None, None),
        P(lead, None),
        P(lead),
    )
    out_specs = (P(lead, None), P(lead, None), P(lead, None, None))
    return jax.shard_map(body, mesh=grid, in_specs=in_specs, out_specs=out_specs, check_vma=False)
```
